32 devices in a mesh: expert: 4 (over y, x), shard: 8 (over z, core).
Axes of the slice: x: 2, y: 2, z: 4, core: 2. Of those that a mesh axis runs over, the one named last changes fastest.
Arguments:
- tokens: bfloat16 [512, 4096], P('expert', 'shard'), may hold values from -6 to 6
- routes: int32 [512, 2], P('expert'), may hold values from 0 to 3, all different within a row; in each aligned block of 128 rows (0 to 127, 128 to 255, ...) at most 128 rows name the same one
- mix_weights: float32 [512, 2], P('expert'), may hold values from 0.1 to 1
- cotangent: bfloat16 [512, 4096], P('expert', 'shard'), may hold values from -6 to 6
- w_gate: bfloat16 [4, 4096, 6144], P('expert', 'shard'), may hold values from -0.09375 to 0.09375
- w_up: bfloat16 [4, 4096, 6144], P('expert', 'shard'), may hold values from -0.09375 to 0.09375
- w_down: bfloat16 [4, 4096, 6144], P('expert', 'shard'), may hold values from -0.078125 to 0.078125
Outputs:
- layer_out: bfloat16 [512, 4096], P('expert', 'shard')
- grad_tokens: bfloat16 [512, 4096], P('expert', 'shard')
- grad_gate: bfloat16 [4, 4096, 6144], P('expert', None, 'shard')
- grad_up: bfloat16 [4, 4096, 6144], P('expert', None, 'shard')
- grad_down: bfloat16 [4, 4096, 6144], P('expert', None, 'shard')
The draws below stay inside these ranges and needn't reach their ends.
Inputs may be any that keep to these rules, and one draw needn't show every extreme that they name: `routes`: each token names two different experts. Among the 128 tokens of one block, no expert is named by more than 128 tokens, and in every draw some expert is named by exactly 128 tokens of some block. Every expert is named by some token.
All inputs are finite; a program needn't handle non-finite values.
Results may differ from the reference program's by a relative error of at most 0.015.
Values may be sent and summed in bfloat16 or wider, within the bound.
A program may use at most 128 MiB of HBM per device.

```python
import math
import jax
import jax.numpy as jnp
import numpy as np
from jax import lax

D = 4096
FFW = 6144
TOK_DEV = 128
EXPERTS = 4
CAP = 128
TOKENS = 512
N_EXPERT = 4
N_SHARD = 8


def block_scale(key, extent, pieces, smallest, largest):
    loudness, own = 1.0, jax.random.fold_in(key, 6)
    for dim, parts in pieces:
        draws = jnp.exp(jax.random.uniform(jax.random.fold_in(own, dim), (parts,), jnp.float32, smallest / len(pieces), largest / len(pieces)))
        loudness = loudness * jnp.repeat(draws, extent[dim] // parts).reshape([-1 if axis == dim else 1 for axis in range(len(extent))])
    return loudness


def deal_out(stream_key, own, number, rows, number_of, top, reach, slope):
    sequence = jax.random.permutation(stream_key, number_of)
    heavy_load, usual = shares(number_of, rows * top, reach, slope, True), shares(number_of, rows * top, reach, slope, False)
    places = jnp.arange(number_of)

    def named(lengths, rotation):
        used = int((lengths > 0).sum())
        fixed = max(1, used // 4)
        shifted = fixed + (places - fixed + rotation * (used - fixed)) % max(1, number_of - fixed)
        return jnp.zeros((number_of,), jnp.int32).at[sequence[jnp.where(places < fixed, places, shifted)]].set(jnp.asarray(lengths, jnp.int32))

    lengths = jnp.where(number % 4 == 0, named(heavy_load, number // 4), named(usual, number - number // 4 - 1))
    mixed = jax.random.permutation(jax.random.fold_in(own, 3), number_of)
    source_of, taker = mixed[0:number_of // 2 * 2:2], mixed[1:number_of // 2 * 2:2]
    room = jnp.minimum(lengths[source_of] - 1, reach - lengths[taker]) // 2
    room = jnp.where((source_of == sequence[0]) | (taker == sequence[0]) | (lengths[taker] == 0), 0, jnp.maximum(room, 0))
    shifted = jax.random.randint(jax.random.fold_in(own, 4), (number_of // 2,), 0, 1 << 20) % (room + 1)
    lengths = lengths.at[source_of].add(-shifted).at[taker].add(shifted)
    labels = jnp.searchsorted(jnp.cumsum(lengths), jnp.arange(rows * top), side="right").astype(jnp.int32)
    table = labels.reshape(top, rows).T
    table = table[jax.random.permutation(jax.random.fold_in(own, 1), rows)]
    rotation = jax.random.randint(jax.random.fold_in(own, 2), (rows, 1), 0, top)
    return jnp.take_along_axis(table, (jnp.arange(top)[None, :] + rotation) % top, axis=1)


def shares(amount, total, most, slope, full):
    weights = [(1 << 20) // math.isqrt(rank ** slope) + 1 for rank in range(1, amount + 1)]
    largest = most if full else min(most, max(-(-total // amount), total * weights[0] // sum(weights)))
    least = 1 if total - largest >= amount - 1 else 0
    counts, spare = [largest] + [least] * (amount - 1), total - largest - least * (amount - 1)
    while spare > 0:
        movable = [i for i in range(1, amount) if counts[i] < largest] or [i for i in range(1, amount) if counts[i] < most]
        mass, left = sum([weights[i] for i in movable]), spare
        for i in movable:
            addition = min(most - counts[i], max(1, left * weights[i] // mass), spare)
            counts[i] = counts[i] + addition
            spare = spare - addition
    return np.array(counts)


def scatter_about(stream_key, shape, deviation, reach, pieces=(), kind=jnp.bfloat16):
    drawn = jax.random.normal(stream_key, shape, jnp.float32) * deviation
    if len(pieces) > 0:
        drawn = block_scale(stream_key, shape, pieces, -0.22, 0.18) * drawn
    return jnp.clip(drawn, min=-reach, max=reach).astype(kind)


def setup_inputs(seed: int = 0) -> dict:
    splits = jax.random.split(jax.random.key(seed), 8)
    tokens = scatter_about(splits[0], (TOKENS, D), 1.0, 6.0, ((0, 4), (1, 8)))
    routes_keys = jax.random.split(jax.random.fold_in(splits[1], 1), TOKENS // TOK_DEV)
    routes_turns = jax.random.permutation(jax.random.fold_in(splits[1], 3), TOKENS // TOK_DEV)
    routes = jax.vmap(lambda own, number: deal_out(jax.random.fold_in(splits[1], 2), own, number, TOK_DEV, EXPERTS, 2, CAP, 2))(routes_keys, routes_turns).reshape((TOKENS, 2))
    mix_weights = jnp.clip(0.1 + 0.9 * jax.random.uniform(splits[2], (TOKENS, 2), jnp.float32) ** block_scale(splits[2], (TOKENS, 2), ((0, 4),), -0.2, 0.2), 0.1, 1.0)
    cotangent = scatter_about(splits[3], (TOKENS, D), 1.0, 6.0, ((0, 4), (1, 8)))
    w_gate = scatter_about(splits[4], (EXPERTS, D, FFW), D ** -0.5, 0.09375, ((0, 4), (1, 8)))
    w_up = scatter_about(splits[5], (EXPERTS, D, FFW), D ** -0.5, 0.09375, ((0, 4), (1, 8)))
    w_down = scatter_about(splits[6], (EXPERTS, D, FFW), FFW ** -0.5, 0.078125, ((0, 4), (1, 8)))
    return dict(tokens=tokens, routes=routes, mix_weights=mix_weights, cotangent=cotangent, w_gate=w_gate, w_up=w_up, w_down=w_down)


def target_rows(routes):
    grouped = routes.reshape(N_EXPERT, TOK_DEV * 2)
    expert_iota = jnp.arange(EXPERTS, dtype=jnp.int32)
    one_hot = (grouped[:, :, None] == expert_iota[None, None, :]).astype(jnp.int32)
    earlier = jnp.cumsum(one_hot, axis=1) - one_hot
    slot_number = jnp.sum(earlier * one_hot, axis=2)
    source = jnp.arange(N_EXPERT, dtype=jnp.int32)[:, None]
    target = grouped * (N_EXPERT * CAP) + source * CAP + slot_number
    return target.reshape(TOKENS, 2).astype(jnp.int32)


def expert_pass(inputs):
    rows_in, grads_in, gate_w, up_w, down_w = inputs
    gate_pre = jnp.dot(rows_in, gate_w, preferred_element_type=jnp.float32)
    up_pre = jnp.dot(rows_in, up_w, preferred_element_type=jnp.float32)
    sigmoid_gate = jax.nn.sigmoid(gate_pre)
    active = gate_pre * sigmoid_gate
    hidden = (active * up_pre).astype(jnp.bfloat16)
    d_hidden = jnp.dot(grads_in, down_w, preferred_element_type=jnp.float32)
    d_gate = (d_hidden * up_pre * sigmoid_gate * (1.0 + gate_pre * (1.0 - sigmoid_gate))).astype(jnp.bfloat16)
    d_up = (d_hidden * active).astype(jnp.bfloat16)
    piece_width = FFW // N_SHARD
    row_count = rows_in.shape[0]

    def one_shard(totals, piece_index):
        carry_out, carry_dx = totals
        first_col = (piece_index * piece_width).astype(jnp.int32)
        hid_piece = lax.dynamic_slice_in_dim(hidden, first_col, piece_width, 1)
        down_piece = lax.dynamic_slice_in_dim(down_w, first_col, piece_width, 1)
        gate_piece = lax.dynamic_slice_in_dim(gate_w, first_col, piece_width, 1)
        up_piece = lax.dynamic_slice_in_dim(up_w, first_col, piece_width, 1)
        dg_piece = lax.dynamic_slice_in_dim(d_gate, first_col, piece_width, 1)
        du_piece = lax.dynamic_slice_in_dim(d_up, first_col, piece_width, 1)
        out_part = jnp.dot(hid_piece, down_piece.T, preferred_element_type=jnp.float32)
        dx_part = jnp.dot(dg_piece, gate_piece.T, preferred_element_type=jnp.float32)
        dx_part = dx_part + jnp.dot(du_piece, up_piece.T, preferred_element_type=jnp.float32)
        out_round = lax.optimization_barrier(out_part.astype(jnp.bfloat16)).astype(jnp.float32)
        dx_round = lax.optimization_barrier(dx_part.astype(jnp.bfloat16)).astype(jnp.float32)
        return (carry_out + out_round, carry_dx + dx_round), None

    zeros_rows = jnp.zeros((row_count, D), jnp.float32)
    totals, unused = lax.scan(one_shard, (zeros_rows, zeros_rows), jnp.arange(N_SHARD, dtype=jnp.int32))
    out_rows = totals[0].astype(jnp.bfloat16)
    dx_rows = totals[1].astype(jnp.bfloat16)
    grad_gate = jnp.dot(rows_in.T, d_gate, preferred_element_type=jnp.float32).astype(jnp.bfloat16)
    grad_up = jnp.dot(rows_in.T, d_up, preferred_element_type=jnp.float32).astype(jnp.bfloat16)
    grad_down = jnp.dot(grads_in.T, hidden, preferred_element_type=jnp.float32).astype(jnp.bfloat16)
    return out_rows, dx_rows, grad_gate, grad_up, grad_down


def reference(tokens, routes, mix_weights, cotangent, w_gate, w_up, w_down):
    target = target_rows(routes)
    flat_target = target.reshape(-1)
    token_index = jnp.repeat(jnp.arange(TOKENS, dtype=jnp.int32), 2)
    total_rows = EXPERTS * N_EXPERT * CAP
    sent_rows = jnp.zeros((total_rows, D), jnp.bfloat16).at[flat_target].set(tokens[token_index])
    scaled = (mix_weights[:, :, None] * cotangent[:, None, :].astype(jnp.float32)).astype(jnp.bfloat16)
    sent_grads = jnp.zeros((total_rows, D), jnp.bfloat16).at[flat_target].set(scaled.reshape(TOKENS * 2, D))
    results = lax.map(expert_pass, (sent_rows.reshape(EXPERTS, N_EXPERT * CAP, D), sent_grads.reshape(EXPERTS, N_EXPERT * CAP, D), w_gate, w_up, w_down))
    out_rows, dx_rows, grad_gate, grad_up, grad_down = results
    picked = out_rows.reshape(total_rows, D)[target]
    layer_out = jnp.sum(mix_weights[:, :, None] * picked.astype(jnp.float32), axis=1).astype(jnp.bfloat16)
    picked_dx = dx_rows.reshape(total_rows, D)[target]
    grad_tokens = jnp.sum(picked_dx.astype(jnp.float32), axis=1).astype(jnp.bfloat16)
    return layer_out, grad_tokens, grad_gate, grad_up, grad_down
```

```python
import functools

import jax
import jax.numpy as jnp
from jax import lax
from jax.experimental import pallas as pl
from jax.experimental.pallas import tpu as pltpu
from jax.sharding import PartitionSpec as P

MESH = pl.DeviceIdType.MESH
VMEM_BUDGET = 56 * 1024 * 1024
ROW_CUTS = 2


def place(shards):
    me = lax.axis_index("shard")
    chip = me // 2
    core = me % 2
    return me, chip, core, me + 1 - 2 * core


def greet(me, chip, sibling, line):
    barrier = pltpu.get_barrier_semaphore()
    pl.semaphore_signal(barrier, inc=1, device_id={"shard": sibling}, device_id_type=MESH)

    @pl.when(chip > 0)
    def _():
        pl.semaphore_signal(barrier, inc=1, device_id={"shard": me - 2}, device_id_type=MESH)

    @pl.when(chip < line - 1)
    def _():
        pl.semaphore_signal(barrier, inc=1, device_id={"shard": me + 2}, device_id_type=MESH)

    peers = jnp.where(chip > 0, 2, 1) + jnp.where(chip < line - 1, 1, 0)
    pl.semaphore_wait(barrier, peers)


def scatter_sum_kernel(
    shards, cuts, p0, p1, p2, out, stage, core_in, line_in,
    load_sem, core_send, core_recv, line_send, line_recv,
):
    line = shards // 2
    units, _, rows, width = stage.shape
    me, chip, core, sibling = place(shards)
    order = sorted(range(line), key=lambda d: -abs(2 * d - line + 1))
    greet(me, chip, sibling, line)

    def load(part, u, r, d):
        cols = pl.ds(pl.multiple_of((2 * d + core) * width, 128), width)
        return pltpu.make_async_copy(
            part.at[pl.ds(r * rows, rows), cols], stage.at[u, d], load_sem.at[u, d]
        )

    def swap(part, u, r, d):
        cols = pl.ds(pl.multiple_of((2 * d + 1 - core) * width, 128), width)
        return pltpu.make_async_remote_copy(
            src_ref=part.at[pl.ds(r * rows, rows), cols],
            dst_ref=core_in.at[u, d],
            send_sem=core_send.at[u, d],
            recv_sem=core_recv.at[u, d],
            device_id={"shard": sibling},
            device_id_type=MESH,
        )

    def pass_on(u, d, slot, to):
        return pltpu.make_async_remote_copy(
            src_ref=stage.at[u, d],
            dst_ref=line_in.at[u, slot],
            send_sem=line_send.at[u, d],
            recv_sem=line_recv.at[u, slot],
            device_id={"shard": to},
            device_id_type=MESH,
        )

    for m, part in enumerate((p0, p1, p2)):
        def begin(r, carry, m=m, part=part):
            u = m * cuts + r
            for d in order:
                swap(part, u, r, d).start()
                load(part, u, r, d).start()
            return carry

        lax.fori_loop(0, cuts, begin, 0)

    def wide(ref):
        return ref[...].astype(jnp.float32)

    def relay(u, carry):
        for d in order:
            @pl.when(chip != d)
            def _(d=d):
                rightward = chip < d
                slot = jnp.where(rightward, d + 1, d)
                to = jnp.where(rightward, me + 2, me - 2)
                load(p0, u, 0, d).wait()
                swap(p0, u, 0, d).wait_recv()
                at_end = jnp.where(rightward, chip == 0, chip == line - 1)

                @pl.when(at_end)
                def _():
                    stage[u, d] = (wide(stage.at[u, d]) + wide(core_in.at[u, d])).astype(
                        stage.dtype
                    )

                @pl.when(jnp.logical_not(at_end))
                def _():
                    pass_on(u, d, slot, to).wait_recv()
                    stage[u, d] = (
                        wide(stage.at[u, d]) + wide(core_in.at[u, d]) + wide(line_in.at[u, slot])
                    ).astype(stage.dtype)

                pass_on(u, d, slot, to).start()
        return carry

    lax.fori_loop(0, units, relay, 0)

    def finish(u, carry):
        load(p0, u, 0, chip).wait()
        swap(p0, u, 0, chip).wait_recv()
        out[u] = wide(stage.at[u, chip]) + wide(core_in.at[u, chip])

        @pl.when(chip > 0)
        def _():
            pass_on(u, chip, chip + 1, sibling).wait_recv()
            out[u] += wide(line_in.at[u, chip + 1])

        @pl.when(chip < line - 1)
        def _():
            pass_on(u, chip, chip, sibling).wait_recv()
            out[u] += wide(line_in.at[u, chip])

        for d in range(line):
            swap(p0, u, 0, d).wait_send()

            @pl.when(chip != d)
            def _(d=d):
                pass_on(u, d, d, sibling).wait_send()
        return carry

    lax.fori_loop(0, units, finish, 0)


def scatter_sum(shards, parts):
    rows_all, cols = parts[0].shape
    rows, width, line = rows_all // ROW_CUTS, cols // shards, shards // 2
    units = 3 * ROW_CUTS
    dma = pltpu.SemaphoreType.DMA
    out = pl.pallas_call(
        functools.partial(scatter_sum_kernel, shards, ROW_CUTS),
        out_shape=jax.ShapeDtypeStruct((units, rows, width), jnp.float32),
        in_specs=[pl.BlockSpec(memory_space=pl.ANY)] * 3,
        out_specs=pl.BlockSpec(memory_space=pltpu.VMEM),
        scratch_shapes=[
            pltpu.VMEM((units, line, rows, width), jnp.bfloat16),
            pltpu.VMEM((units, line, rows, width), jnp.bfloat16),
            pltpu.VMEM((units, line + 1, rows, width), jnp.bfloat16),
            dma((units, line)),
            dma((units, line)),
            dma((units, line)),
            dma((units, line)),
            dma((units, line + 1)),
        ],
        compiler_params=pltpu.CompilerParams(
            collective_id=0, has_side_effects=True, vmem_limit_bytes=VMEM_BUDGET
        ),
        cost_estimate=pl.CostEstimate(
            flops=100_000_000_000, bytes_accessed=500_000_000, transcendentals=0
        ),
    )(*parts)
    return out.reshape(3, rows_all, width)


def gather_kernel(shards, cuts, a, b, c, full, own_sem, line_right, line_left, line_recv, core_send, core_recv):
    line = shards // 2
    rows_all, width = a.shape
    rows = rows_all // cuts
    units = 3 * cuts
    me, chip, core, sibling = place(shards)
    greet(me, chip, sibling, line)

    def block(u, shard):
        return full.at[
            pl.ds(u * rows, rows), pl.ds(pl.multiple_of(shard * width, 128), width)
        ]

    def send(src, u, origin, way):
        shard = 2 * origin + core
        return pltpu.make_async_remote_copy(
            src_ref=src,
            dst_ref=block(u, shard),
            send_sem=(line_right if way > 0 else line_left).at[u, origin],
            recv_sem=line_recv.at[u, origin],
            device_id={"shard": me + 2 * way},
            device_id_type=MESH,
        )

    def share(src, u, origin):
        return pltpu.make_async_remote_copy(
            src_ref=src,
            dst_ref=block(u, 2 * origin + core),
            send_sem=core_send.at[u, origin],
            recv_sem=core_recv.at[u, origin],
            device_id={"shard": sibling},
            device_id_type=MESH,
        )

    for m, part in enumerate((a, b, c)):
        def begin(r, carry, m=m, part=part):
            u = m * cuts + r
            src = part.at[pl.ds(r * rows, rows)]

            @pl.when(chip < line - 1)
            def _():
                send(src, u, chip, 1).start()

            @pl.when(chip > 0)
            def _():
                send(src, u, chip, -1).start()

            share(src, u, chip).start()
            pltpu.make_async_copy(src, block(u, me), own_sem.at[u]).start()
            return carry

        lax.fori_loop(0, cuts, begin, 0)

    for step in range(1, line):
        def relay(u, carry, step=step):
            @pl.when(chip - step >= 0)
            def _():
                origin = chip - step
                got = block(u, 2 * origin + core)
                send(got, u, origin, 1).wait_recv()

                @pl.when(chip < line - 1)
                def _():
                    send(got, u, origin, 1).start()

                share(got, u, origin).start()

            @pl.when(chip + step < line)
            def _():
                origin = chip + step
                got = block(u, 2 * origin + core)
                send(got, u, origin, -1).wait_recv()

                @pl.when(chip > 0)
                def _():
                    send(got, u, origin, -1).start()

                share(got, u, origin).start()
            return carry

        lax.fori_loop(0, units, relay, 0)

    def finish(u, carry):
        pltpu.make_async_copy(a.at[pl.ds(0, rows)], block(u, me), own_sem.at[u]).wait()
        for d in range(line):
            got = block(u, 2 * d + core)
            share(got, u, d).wait()

            @pl.when(jnp.logical_and(d <= chip, chip < line - 1))
            def _(d=d, got=got):
                send(got, u, d, 1).wait_send()

            @pl.when(jnp.logical_and(d >= chip, chip > 0))
            def _(d=d, got=got):
                send(got, u, d, -1).wait_send()
        return carry

    lax.fori_loop(0, units, finish, 0)


def gather_all(shards, parts):
    rows_all, width = parts[0].shape
    line = shards // 2
    units = 3 * ROW_CUTS
    dma = pltpu.SemaphoreType.DMA
    return pl.pallas_call(
        functools.partial(gather_kernel, shards, ROW_CUTS),
        out_shape=jax.ShapeDtypeStruct((3 * rows_all, shards * width), jnp.bfloat16),
        in_specs=[pl.BlockSpec(memory_space=pl.ANY)] * 3,
        out_specs=pl.BlockSpec(memory_space=pl.ANY),
        scratch_shapes=[
            dma((units,)),
            dma((units, line)),
            dma((units, line)),
            dma((units, line)),
            dma((units, line)),
            dma((units, line)),
        ],
        compiler_params=pltpu.CompilerParams(
            collective_id=1, has_side_effects=True, vmem_limit_bytes=VMEM_BUDGET
        ),
        cost_estimate=pl.CostEstimate(
            flops=100_000_000_000, bytes_accessed=500_000_000, transcendentals=0
        ),
    )(*parts)


def use_kernels(shards, rows, cols):
    line = shards // 2
    chunk = 3 * rows * (cols // shards)
    need = chunk * (2 * (3 * line + 1) + 4)
    return shards % 2 == 0 and shards > 2 and need < VMEM_BUDGET - 8 * 1024 * 1024


def to_hidden_slices(parts):
    shards = lax.axis_size("shard")
    if use_kernels(shards, *parts[0].shape):
        return scatter_sum(shards, parts)
    return tuple(
        lax.psum_scatter(part, "shard", scatter_dimension=1, tiled=True).astype(jnp.float32)
        for part in parts
    )


def to_all_hidden(slices):
    shards = lax.axis_size("shard")
    rows, width = slices[0].shape
    if use_kernels(shards, rows, width * shards):
        full = gather_all(shards, slices)
        return full[:rows], full[rows : 2 * rows], full[2 * rows :]
    return tuple(lax.all_gather(part, "shard", axis=1, tiled=True) for part in slices)


def send_home(rows):
    experts = lax.axis_size("expert")
    shaped = rows.reshape(experts, rows.shape[0] // experts, rows.shape[1])
    return lax.all_to_all(shaped, "expert", split_axis=0, concat_axis=0, tiled=True)


def local(tokens, routes, mix_weights, cotangent, w_gate, w_up, w_down):
    experts = lax.axis_size("expert")
    expert = lax.axis_index("expert")
    w_gate, w_up, w_down = w_gate[0], w_up[0], w_down[0]

    routes_all = lax.all_gather(routes, "expert", axis=0, tiled=True)
    mix_all = lax.all_gather(mix_weights, "expert", axis=0, tiled=True)
    row_weight = jnp.sum(jnp.where(routes_all == expert, mix_all, 0.0), axis=1)[:, None]
    home_weight = jnp.sum(
        jnp.where(
            routes[None, :, :] == jnp.arange(experts, dtype=routes.dtype)[:, None, None],
            mix_weights[None, :, :],
            0.0,
        ),
        axis=2,
    )

    x_part = lax.all_gather(tokens, "expert", axis=0, tiled=True)
    cot_part = lax.all_gather(cotangent, "expert", axis=0, tiled=True)
    dy_part = (row_weight * cot_part.astype(jnp.float32)).astype(jnp.bfloat16)

    def partial(rows, weights):
        return jnp.dot(rows, weights, preferred_element_type=jnp.float32).astype(jnp.bfloat16)

    gate_pre, up_pre, d_hidden = to_hidden_slices(
        (partial(x_part, w_gate), partial(x_part, w_up), partial(dy_part, w_down))
    )

    sigmoid_gate = jax.nn.sigmoid(gate_pre)
    active = gate_pre * sigmoid_gate
    hidden = (active * up_pre).astype(jnp.bfloat16)
    d_gate = (d_hidden * up_pre * sigmoid_gate * (1.0 + gate_pre * (1.0 - sigmoid_gate))).astype(
        jnp.bfloat16
    )
    d_up = (d_hidden * active).astype(jnp.bfloat16)

    hidden_all, d_gate_all, d_up_all = to_all_hidden((hidden, d_gate, d_up))
    col_contract = (((1,), (1,)), ((), ()))
    out_rows = lax.dot_general(
        hidden_all, w_down, col_contract, preferred_element_type=jnp.float32
    ).astype(jnp.bfloat16)
    dx_rows = lax.dot_general(d_gate_all, w_gate, col_contract, preferred_element_type=jnp.float32)
    dx_rows = dx_rows + lax.dot_general(
        d_up_all, w_up, col_contract, preferred_element_type=jnp.float32
    )
    dx_rows = dx_rows.astype(jnp.bfloat16)
    out_home = send_home(out_rows)
    dx_home = send_home(dx_rows)
    layer_out = jnp.sum(home_weight[:, :, None] * out_home.astype(jnp.float32), axis=0).astype(
        jnp.bfloat16
    )
    grad_tokens = jnp.sum(dx_home.astype(jnp.float32), axis=0).astype(jnp.bfloat16)

    x_rows = lax.all_gather(
        lax.all_gather(tokens, "shard", axis=1, tiled=True), "expert", axis=0, tiled=True
    )
    cot_rows = lax.all_gather(
        lax.all_gather(cotangent, "shard", axis=1, tiled=True), "expert", axis=0, tiled=True
    )
    dy_rows = (row_weight * cot_rows.astype(jnp.float32)).astype(jnp.bfloat16)
    row_contract = (((0,), (0,)), ((), ()))

    def gradient(rows, slices):
        return lax.dot_general(
            rows, slices, row_contract, preferred_element_type=jnp.float32
        ).astype(jnp.bfloat16)

    grad_down = gradient(dy_rows, hidden)
    grad_gate = gradient(x_rows, d_gate)
    grad_up = gradient(x_rows, d_up)
    return (layer_out, grad_tokens, grad_gate[None], grad_up[None], grad_down[None])


def solution(mesh):
    return jax.shard_map(
        local,
        mesh=mesh,
        in_specs=(
            P("expert", "shard"),
            P("expert", None),
            P("expert", None),
            P("expert", "shard"),
            P("expert", "shard", None),
            P("expert", "shard", None),
            P("expert", "shard", None),
        ),
        out_specs=(
            P("expert", "shard"),
            P("expert", "shard"),
            P("expert", None, "shard"),
            P("expert", None, "shard"),
            P("expert", None, "shard"),
        ),
        check_vma=False,
    )
```

```python
import functools

import jax
import jax.numpy as jnp
from jax import lax
from jax.experimental import pallas as pl
from jax.experimental.pallas import tpu as pltpu
from jax.sharding import PartitionSpec as P

MESH = pl.DeviceIdType.MESH
VMEM_BUDGET = 56 * 1024 * 1024
BLOCKS = 8


def place(shards):
    me = lax.axis_index("shard")
    chip = me // 2
    core = me % 2
    return me, chip, core, me + 1 - 2 * core


def greet(me, chip, sibling, line):
    barrier = pltpu.get_barrier_semaphore()
    pl.semaphore_signal(barrier, inc=1, device_id={"shard": sibling}, device_id_type=MESH)

    @pl.when(chip > 0)
    def _():
        pl.semaphore_signal(barrier, inc=1, device_id={"shard": me - 2}, device_id_type=MESH)

    @pl.when(chip < line - 1)
    def _():
        pl.semaphore_signal(barrier, inc=1, device_id={"shard": me + 2}, device_id_type=MESH)

    peers = jnp.where(chip > 0, 2, 1) + jnp.where(chip < line - 1, 1, 0)
    pl.semaphore_wait(barrier, peers)


def exchange_kernel(
    shards, blocks, p0, p1, p2, mine, full, stage, core_in, line_in,
    load_sem, core_send, core_recv, line_send, line_recv,
    ring_right, ring_left, ring_recv, pair_send, pair_recv, own_sem,
):
    line = shards // 2
    rows, width = stage.shape[3], stage.shape[4]
    me, chip, core, sibling = place(shards)
    left_half = 2 * chip < line
    greet(me, chip, sibling, line)

    def rows_of(r):
        return pl.ds(pl.multiple_of(r * rows, rows), rows)

    def cols_of(shard):
        return pl.ds(pl.multiple_of(shard * width, 128), width)

    def turn(j):
        return jnp.where(left_half, line - 1 - j, j)

    def load(part, r, d, m):
        return pltpu.make_async_copy(
            part.at[rows_of(r), cols_of(2 * d + core)], stage.at[r, d, m], load_sem.at[r, d, m]
        )

    def swap(part, r, d, m):
        return pltpu.make_async_remote_copy(
            src_ref=part.at[rows_of(r), cols_of(2 * d + 1 - core)],
            dst_ref=core_in.at[r, d, m],
            send_sem=core_send.at[r, d, m],
            recv_sem=core_recv.at[r, d, m],
            device_id={"shard": sibling},
            device_id_type=MESH,
        )

    def pass_on(r, d, slot, to):
        return pltpu.make_async_remote_copy(
            src_ref=stage.at[r, d],
            dst_ref=line_in.at[r, slot],
            send_sem=line_send.at[r, d],
            recv_sem=line_recv.at[r, slot],
            device_id={"shard": to},
            device_id_type=MESH,
        )

    def block(r, shard):
        return full.at[:, rows_of(r), cols_of(shard)]

    def send(src, r, origin, way):
        return pltpu.make_async_remote_copy(
            src_ref=src,
            dst_ref=block(r, 2 * origin + core),
            send_sem=(ring_right if way > 0 else ring_left).at[r, origin],
            recv_sem=ring_recv.at[r, origin],
            device_id={"shard": me + 2 * way},
            device_id_type=MESH,
        )

    def share(src, r, origin):
        return pltpu.make_async_remote_copy(
            src_ref=src,
            dst_ref=block(r, 2 * origin + core),
            send_sem=pair_send.at[r, origin],
            recv_sem=pair_recv.at[r, origin],
            device_id={"shard": sibling},
            device_id_type=MESH,
        )

    def keep(r):
        return pltpu.make_async_copy(mine.at[:, rows_of(r)], block(r, me), own_sem.at[r])

    def wide(value):
        return value.astype(jnp.float32)

    def begin(r):
        for j in range(line):
            for m, part in enumerate((p0, p1, p2)):
                swap(part, r, turn(j), m).start()
                load(part, r, turn(j), m).start()

    def arrived(r, d):
        for m in range(3):
            load(p0, r, d, m).wait()
            swap(p0, r, d, m).wait_recv()

    def relay(r):
        for j in range(line):
            d = turn(j)

            @pl.when(chip != d)
            def _(d=d):
                rightward = chip < d
                slot = jnp.where(rightward, d + 1, d)
                to = jnp.where(rightward, me + 2, me - 2)
                at_end = jnp.where(rightward, chip, line - 1 - chip) == 0
                arrived(r, d)

                @pl.when(at_end)
                def _():
                    for m in range(3):
                        stage[r, d, m] = (wide(stage[r, d, m]) + wide(core_in[r, d, m])).astype(
                            stage.dtype
                        )

                @pl.when(jnp.logical_not(at_end))
                def _():
                    pass_on(r, d, slot, to).wait_recv()
                    for m in range(3):
                        stage[r, d, m] = (
                            wide(stage[r, d, m]) + wide(core_in[r, d, m]) + wide(line_in[r, slot, m])
                        ).astype(stage.dtype)

                pass_on(r, d, slot, to).start()

    def finish(r):
        arrived(r, chip)

        def total(m):
            return wide(stage[r, chip, m]) + wide(core_in[r, chip, m])

        def store(gate_pre, up_pre, d_hidden):
            sigmoid_gate = jax.nn.sigmoid(gate_pre)
            active = gate_pre * sigmoid_gate
            slope = sigmoid_gate * (1.0 + gate_pre * (1.0 - sigmoid_gate))
            mine[0, rows_of(r)] = (active * up_pre).astype(mine.dtype)
            mine[1, rows_of(r)] = (d_hidden * up_pre * slope).astype(mine.dtype)
            mine[2, rows_of(r)] = (d_hidden * active).astype(mine.dtype)

        @pl.when(chip == 0)
        def _():
            pass_on(r, chip, chip, sibling).wait_recv()
            store(*[total(m) + wide(line_in[r, chip, m]) for m in range(3)])

        @pl.when(chip == line - 1)
        def _():
            pass_on(r, chip, chip + 1, sibling).wait_recv()
            store(*[total(m) + wide(line_in[r, chip + 1, m]) for m in range(3)])

        @pl.when(jnp.logical_and(chip > 0, chip < line - 1))
        def _():
            pass_on(r, chip, chip, sibling).wait_recv()
            pass_on(r, chip, chip + 1, sibling).wait_recv()
            store(
                *[
                    total(m) + wide(line_in[r, chip, m]) + wide(line_in[r, chip + 1, m])
                    for m in range(3)
                ]
            )

        src = mine.at[:, rows_of(r)]

        @pl.when(chip < line - 1)
        def _():
            send(src, r, chip, 1).start()

        @pl.when(chip > 0)
        def _():
            send(src, r, chip, -1).start()

        share(src, r, chip).start()
        keep(r).start()

    def forward(r, step):
        @pl.when(chip - step >= 0)
        def _():
            origin = chip - step
            got = block(r, 2 * origin + core)
            send(got, r, origin, 1).wait_recv()

            @pl.when(chip < line - 1)
            def _():
                send(got, r, origin, 1).start()

            share(got, r, origin).start()

        @pl.when(chip + step < line)
        def _():
            origin = chip + step
            got = block(r, 2 * origin + core)
            send(got, r, origin, -1).wait_recv()

            @pl.when(chip > 0)
            def _():
                send(got, r, origin, -1).start()

            share(got, r, origin).start()

    begin(0)

    def advance(i, carry):
        @pl.when(i + 1 < blocks)
        def _():
            begin(i + 1)

        @pl.when(i < blocks)
        def _():
            relay(i)

        @pl.when(jnp.logical_and(i >= 1, i - 1 < blocks))
        def _():
            finish(i - 1)

        for step in range(1, line):
            @pl.when(jnp.logical_and(i >= 1 + step, i - 1 - step < blocks))
            def _(step=step):
                forward(i - 1 - step, step)
        return carry

    lax.fori_loop(0, blocks + line, advance, 0)

    def settle(r, carry):
        keep(r).wait()
        for d in range(line):
            got = block(r, 2 * d + core)
            share(got, r, d).wait()
            for m in range(3):
                swap(p0, r, d, m).wait_send()

            @pl.when(chip != d)
            def _(d=d):
                pass_on(r, d, d, sibling).wait_send()

            @pl.when(jnp.logical_and(d <= chip, chip < line - 1))
            def _(d=d, got=got):
                send(got, r, d, 1).wait_send()

            @pl.when(jnp.logical_and(d >= chip, chip > 0))
            def _(d=d, got=got):
                send(got, r, d, -1).wait_send()
        return carry

    lax.fori_loop(0, blocks, settle, 0)


def exchange(shards, parts):
    rows_all, cols = parts[0].shape
    rows, width, line = rows_all // BLOCKS, cols // shards, shards // 2
    dma = pltpu.SemaphoreType.DMA
    pairs, triples = (BLOCKS, line), (BLOCKS, line, 3)
    chunks = (BLOCKS, line, 3, rows, width)
    return pl.pallas_call(
        functools.partial(exchange_kernel, shards, BLOCKS),
        out_shape=(
            jax.ShapeDtypeStruct((3, rows_all, width), jnp.bfloat16),
            jax.ShapeDtypeStruct((3, rows_all, cols), jnp.bfloat16),
        ),
        in_specs=[pl.BlockSpec(memory_space=pl.ANY)] * 3,
        out_specs=(pl.BlockSpec(memory_space=pltpu.VMEM), pl.BlockSpec(memory_space=pl.ANY)),
        scratch_shapes=[
            pltpu.VMEM(chunks, jnp.bfloat16),
            pltpu.VMEM(chunks, jnp.bfloat16),
            pltpu.VMEM((BLOCKS, line + 1, 3, rows, width), jnp.bfloat16),
            dma(triples),
            dma(triples),
            dma(triples),
            dma(pairs),
            dma((BLOCKS, line + 1)),
            dma(pairs),
            dma(pairs),
            dma(pairs),
            dma(pairs),
            dma(pairs),
            dma((BLOCKS,)),
        ],
        compiler_params=pltpu.CompilerParams(
            collective_id=0, has_side_effects=True, vmem_limit_bytes=VMEM_BUDGET
        ),
        cost_estimate=pl.CostEstimate(
            flops=200_000_000_000, bytes_accessed=800_000_000, transcendentals=0
        ),
    )(*parts)


def use_kernels(shards, rows, cols):
    line = shards // 2
    chunk = 3 * rows * (cols // shards)
    need = chunk * (2 * (3 * line + 1) + 4)
    return shards % 2 == 0 and shards > 2 and need < VMEM_BUDGET - 8 * 1024 * 1024


def activate(gate_pre, up_pre, d_hidden):
    sigmoid_gate = jax.nn.sigmoid(gate_pre)
    active = gate_pre * sigmoid_gate
    hidden = active * up_pre
    d_gate = d_hidden * up_pre * sigmoid_gate * (1.0 + gate_pre * (1.0 - sigmoid_gate))
    return tuple(value.astype(jnp.bfloat16) for value in (hidden, d_gate, d_hidden * active))


def to_hidden(parts):
    shards = lax.axis_size("shard")
    if use_kernels(shards, *parts[0].shape):
        return exchange(shards, parts)
    sums = [
        lax.psum_scatter(part, "shard", scatter_dimension=1, tiled=True).astype(jnp.float32)
        for part in parts
    ]
    mine = activate(*sums)
    return mine, tuple(lax.all_gather(part, "shard", axis=1, tiled=True) for part in mine)


def send_home(rows):
    experts = lax.axis_size("expert")
    shaped = rows.reshape(experts, rows.shape[0] // experts, rows.shape[1])
    return lax.all_to_all(shaped, "expert", split_axis=0, concat_axis=0, tiled=True)


def local(tokens, routes, mix_weights, cotangent, w_gate, w_up, w_down):
    experts = lax.axis_size("expert")
    w_gate, w_up, w_down = w_gate[0], w_up[0], w_down[0]

    home_weight = jnp.sum(
        jnp.where(
            routes[None, :, :] == jnp.arange(experts, dtype=routes.dtype)[:, None, None],
            mix_weights[None, :, :],
            0.0,
        ),
        axis=2,
    )
    features = tokens.shape[1]
    dy_home = (home_weight[:, :, None] * cotangent.astype(jnp.float32)[None]).astype(jnp.bfloat16)
    sent = jnp.concatenate([jnp.broadcast_to(tokens[None], dy_home.shape), dy_home], axis=2)
    got = lax.all_to_all(sent, "expert", split_axis=0, concat_axis=0, tiled=True)
    got = got.reshape(-1, 2 * features)
    x_part, dy_part = got[:, :features], got[:, features:]
    row_weight = lax.all_to_all(
        home_weight[:, None, :], "expert", split_axis=0, concat_axis=0, tiled=True
    ).reshape(-1, 1)

    def partial(rows, weights):
        return jnp.dot(rows, weights, preferred_element_type=jnp.float32).astype(jnp.bfloat16)

    (hidden, d_gate, d_up), (hidden_all, d_gate_all, d_up_all) = to_hidden(
        (partial(x_part, w_gate), partial(x_part, w_up), partial(dy_part, w_down))
    )
    col_contract = (((1,), (1,)), ((), ()))
    out_rows = lax.dot_general(
        hidden_all, w_down, col_contract, preferred_element_type=jnp.float32
    ).astype(jnp.bfloat16)
    dx_rows = lax.dot_general(d_gate_all, w_gate, col_contract, preferred_element_type=jnp.float32)
    dx_rows = dx_rows + lax.dot_general(
        d_up_all, w_up, col_contract, preferred_element_type=jnp.float32
    )
    dx_rows = dx_rows.astype(jnp.bfloat16)
    out_home = send_home(out_rows)
    dx_home = send_home(dx_rows)
    layer_out = jnp.sum(home_weight[:, :, None] * out_home.astype(jnp.float32), axis=0).astype(
        jnp.bfloat16
    )
    grad_tokens = jnp.sum(dx_home.astype(jnp.float32), axis=0).astype(jnp.bfloat16)

    x_rows = lax.all_gather(
        lax.all_gather(tokens, "shard", axis=1, tiled=True), "expert", axis=0, tiled=True
    )
    x_rows = jnp.where(row_weight > 0, x_rows, jnp.zeros_like(x_rows))
    cot_rows = lax.all_gather(
        lax.all_gather(cotangent, "shard", axis=1, tiled=True), "expert", axis=0, tiled=True
    )
    dy_rows = (row_weight * cot_rows.astype(jnp.float32)).astype(jnp.bfloat16)
    row_contract = (((0,), (0,)), ((), ()))

    def gradient(rows, slices):
        return lax.dot_general(
            rows, slices, row_contract, preferred_element_type=jnp.float32
        ).astype(jnp.bfloat16)

    grad_down = gradient(dy_rows, hidden)
    grad_gate = gradient(x_rows, d_gate)
    grad_up = gradient(x_rows, d_up)
    return (layer_out, grad_tokens, grad_gate[None], grad_up[None], grad_down[None])


def solution(mesh):
    return jax.shard_map(
        local,
        mesh=mesh,
        in_specs=(
            P("expert", "shard"),
            P("expert", None),
            P("expert", None),
            P("expert", "shard"),
            P("expert", "shard", None),
            P("expert", "shard", None),
            P("expert", "shard", None),
        ),
        out_specs=(
            P("expert", "shard"),
            P("expert", "shard"),
            P("expert", None, "shard"),
            P("expert", None, "shard"),
            P("expert", None, "shard"),
        ),
        check_vma=False,
    )
```

```python
import functools

import jax
import jax.numpy as jnp
from jax import lax
from jax.experimental import pallas as pl
from jax.experimental.pallas import tpu as pltpu
from jax.sharding import PartitionSpec as P

MESH = pl.DeviceIdType.MESH
VMEM_BUDGET = 56 * 1024 * 1024
BLOCKS = 16
LAG = 2


def place(shards):
    me = lax.axis_index("shard")
    chip = me // 2
    core = me % 2
    return me, chip, core, me + 1 - 2 * core


def greet(me, chip, sibling, line):
    barrier = pltpu.get_barrier_semaphore()
    pl.semaphore_signal(barrier, inc=1, device_id={"shard": sibling}, device_id_type=MESH)

    @pl.when(chip > 0)
    def _():
        pl.semaphore_signal(barrier, inc=1, device_id={"shard": me - 2}, device_id_type=MESH)

    @pl.when(chip < line - 1)
    def _():
        pl.semaphore_signal(barrier, inc=1, device_id={"shard": me + 2}, device_id_type=MESH)

    peers = jnp.where(chip > 0, 2, 1) + jnp.where(chip < line - 1, 1, 0)
    pl.semaphore_wait(barrier, peers)


def exchange_kernel(
    shards, blocks, p0, p1, p2, mine, full, stage, core_in, line_in,
    load_sem, core_send, core_recv, line_send, line_recv,
    ring_right, ring_left, ring_recv, pair_send, pair_recv, own_sem,
):
    line = shards // 2
    rows, width = stage.shape[3], stage.shape[4]
    me, chip, core, sibling = place(shards)
    left_half = 2 * chip < line
    greet(me, chip, sibling, line)

    def rows_of(r):
        return pl.ds(pl.multiple_of(r * rows, rows), rows)

    def cols_of(shard):
        return pl.ds(pl.multiple_of(shard * width, 128), width)

    def turn(j):
        return jnp.where(left_half, line - 1 - j, j)

    def load(part, r, d, m):
        return pltpu.make_async_copy(
            part.at[rows_of(r), cols_of(2 * d + core)], stage.at[r, d, m], load_sem.at[r, d, m]
        )

    def swap(part, r, d, m):
        return pltpu.make_async_remote_copy(
            src_ref=part.at[rows_of(r), cols_of(2 * d + 1 - core)],
            dst_ref=core_in.at[r, d, m],
            send_sem=core_send.at[r, d, m],
            recv_sem=core_recv.at[r, d, m],
            device_id={"shard": sibling},
            device_id_type=MESH,
        )

    def pass_on(r, d, slot, to):
        return pltpu.make_async_remote_copy(
            src_ref=stage.at[r, d],
            dst_ref=line_in.at[r, slot],
            send_sem=line_send.at[r, d],
            recv_sem=line_recv.at[r, slot],
            device_id={"shard": to},
            device_id_type=MESH,
        )

    def block(r, shard):
        return full.at[:, rows_of(r), cols_of(shard)]

    def send(src, r, origin, way):
        return pltpu.make_async_remote_copy(
            src_ref=src,
            dst_ref=block(r, 2 * origin + core),
            send_sem=(ring_right if way > 0 else ring_left).at[r, origin],
            recv_sem=ring_recv.at[r, origin],
            device_id={"shard": me + 2 * way},
            device_id_type=MESH,
        )

    def share(src, r, origin):
        return pltpu.make_async_remote_copy(
            src_ref=src,
            dst_ref=block(r, 2 * origin + core),
            send_sem=pair_send.at[r, origin],
            recv_sem=pair_recv.at[r, origin],
            device_id={"shard": sibling},
            device_id_type=MESH,
        )

    def keep(r):
        return pltpu.make_async_copy(mine.at[:, rows_of(r)], block(r, me), own_sem.at[r])

    def wide(value):
        return value.astype(jnp.float32)

    def begin(r):
        for j in range(line):
            for m, part in enumerate((p0, p1, p2)):
                swap(part, r, turn(j), m).start()
                load(part, r, turn(j), m).start()

    def arrived(r, d):
        for m in range(3):
            load(p0, r, d, m).wait()
            swap(p0, r, d, m).wait_recv()

    def relay(r):
        for j in range(line):
            d = turn(j)

            @pl.when(chip != d)
            def _(d=d):
                rightward = chip < d
                slot = jnp.where(rightward, d + 1, d)
                to = jnp.where(rightward, me + 2, me - 2)
                at_end = jnp.where(rightward, chip, line - 1 - chip) == 0
                arrived(r, d)

                @pl.when(at_end)
                def _():
                    for m in range(3):
                        stage[r, d, m] = (wide(stage[r, d, m]) + wide(core_in[r, d, m])).astype(
                            stage.dtype
                        )

                @pl.when(jnp.logical_not(at_end))
                def _():
                    pass_on(r, d, slot, to).wait_recv()
                    for m in range(3):
                        stage[r, d, m] = (
                            wide(stage[r, d, m]) + wide(core_in[r, d, m]) + wide(line_in[r, slot, m])
                        ).astype(stage.dtype)

                pass_on(r, d, slot, to).start()

    def finish(r):
        arrived(r, chip)

        def total(m):
            return wide(stage[r, chip, m]) + wide(core_in[r, chip, m])

        def store(gate_pre, up_pre, d_hidden):
            sigmoid_gate = jax.nn.sigmoid(gate_pre)
            active = gate_pre * sigmoid_gate
            slope = sigmoid_gate * (1.0 + gate_pre * (1.0 - sigmoid_gate))
            mine[0, rows_of(r)] = (active * up_pre).astype(mine.dtype)
            mine[1, rows_of(r)] = (d_hidden * up_pre * slope).astype(mine.dtype)
            mine[2, rows_of(r)] = (d_hidden * active).astype(mine.dtype)

        @pl.when(chip == 0)
        def _():
            pass_on(r, chip, chip, sibling).wait_recv()
            store(*[total(m) + wide(line_in[r, chip, m]) for m in range(3)])

        @pl.when(chip == line - 1)
        def _():
            pass_on(r, chip, chip + 1, sibling).wait_recv()
            store(*[total(m) + wide(line_in[r, chip + 1, m]) for m in range(3)])

        @pl.when(jnp.logical_and(chip > 0, chip < line - 1))
        def _():
            pass_on(r, chip, chip, sibling).wait_recv()
            pass_on(r, chip, chip + 1, sibling).wait_recv()
            store(
                *[
                    total(m) + wide(line_in[r, chip, m]) + wide(line_in[r, chip + 1, m])
                    for m in range(3)
                ]
            )

        src = mine.at[:, rows_of(r)]

        @pl.when(chip < line - 1)
        def _():
            send(src, r, chip, 1).start()

        @pl.when(chip > 0)
        def _():
            send(src, r, chip, -1).start()

        share(src, r, chip).start()
        keep(r).start()

    def forward(r, step):
        @pl.when(chip - step >= 0)
        def _():
            origin = chip - step
            got = block(r, 2 * origin + core)
            send(got, r, origin, 1).wait_recv()

            @pl.when(chip < line - 1)
            def _():
                send(got, r, origin, 1).start()

            share(got, r, origin).start()

        @pl.when(chip + step < line)
        def _():
            origin = chip + step
            got = block(r, 2 * origin + core)
            send(got, r, origin, -1).wait_recv()

            @pl.when(chip > 0)
            def _():
                send(got, r, origin, -1).start()

            share(got, r, origin).start()

    begin(0)

    def advance(i, carry):
        @pl.when(i + 1 < blocks)
        def _():
            begin(i + 1)

        @pl.when(i < blocks)
        def _():
            relay(i)

        @pl.when(jnp.logical_and(i >= LAG, i - LAG < blocks))
        def _():
            finish(i - LAG)

        for step in range(1, line):
            @pl.when(jnp.logical_and(i >= LAG + step, i - LAG - step < blocks))
            def _(step=step):
                forward(i - LAG - step, step)
        return carry

    lax.fori_loop(0, blocks + LAG + line - 1, advance, 0)

    def settle(r, carry):
        keep(r).wait()
        for d in range(line):
            got = block(r, 2 * d + core)
            share(got, r, d).wait()
            for m in range(3):
                swap(p0, r, d, m).wait_send()

            @pl.when(chip != d)
            def _(d=d):
                pass_on(r, d, d, sibling).wait_send()

            @pl.when(jnp.logical_and(d <= chip, chip < line - 1))
            def _(d=d, got=got):
                send(got, r, d, 1).wait_send()

            @pl.when(jnp.logical_and(d >= chip, chip > 0))
            def _(d=d, got=got):
                send(got, r, d, -1).wait_send()
        return carry

    lax.fori_loop(0, blocks, settle, 0)


def exchange(shards, parts):
    rows_all, cols = parts[0].shape
    rows, width, line = rows_all // BLOCKS, cols // shards, shards // 2
    dma = pltpu.SemaphoreType.DMA
    pairs, triples = (BLOCKS, line), (BLOCKS, line, 3)
    chunks = (BLOCKS, line, 3, rows, width)
    return pl.pallas_call(
        functools.partial(exchange_kernel, shards, BLOCKS),
        out_shape=(
            jax.ShapeDtypeStruct((3, rows_all, width), jnp.bfloat16),
            jax.ShapeDtypeStruct((3, rows_all, cols), jnp.bfloat16),
        ),
        in_specs=[pl.BlockSpec(memory_space=pl.ANY)] * 3,
        out_specs=(pl.BlockSpec(memory_space=pltpu.VMEM), pl.BlockSpec(memory_space=pl.ANY)),
        scratch_shapes=[
            pltpu.VMEM(chunks, jnp.bfloat16),
            pltpu.VMEM(chunks, jnp.bfloat16),
            pltpu.VMEM((BLOCKS, line + 1, 3, rows, width), jnp.bfloat16),
            dma(triples),
            dma(triples),
            dma(triples),
            dma(pairs),
            dma((BLOCKS, line + 1)),
            dma(pairs),
            dma(pairs),
            dma(pairs),
            dma(pairs),
            dma(pairs),
            dma((BLOCKS,)),
        ],
        compiler_params=pltpu.CompilerParams(
            collective_id=0, has_side_effects=True, vmem_limit_bytes=VMEM_BUDGET
        ),
        cost_estimate=pl.CostEstimate(
            flops=200_000_000_000, bytes_accessed=800_000_000, transcendentals=0
        ),
    )(*parts)


def use_kernels(shards, rows, cols):
    line = shards // 2
    chunk = 3 * rows * (cols // shards)
    need = chunk * (2 * (3 * line + 1) + 4)
    return shards % 2 == 0 and shards > 2 and need < VMEM_BUDGET - 8 * 1024 * 1024


def activate(gate_pre, up_pre, d_hidden):
    sigmoid_gate = jax.nn.sigmoid(gate_pre)
    active = gate_pre * sigmoid_gate
    hidden = active * up_pre
    d_gate = d_hidden * up_pre * sigmoid_gate * (1.0 + gate_pre * (1.0 - sigmoid_gate))
    return tuple(value.astype(jnp.bfloat16) for value in (hidden, d_gate, d_hidden * active))


def to_hidden(parts):
    shards = lax.axis_size("shard")
    if use_kernels(shards, *parts[0].shape):
        return exchange(shards, parts)
    sums = [
        lax.psum_scatter(part, "shard", scatter_dimension=1, tiled=True).astype(jnp.float32)
        for part in parts
    ]
    mine = activate(*sums)
    return mine, tuple(lax.all_gather(part, "shard", axis=1, tiled=True) for part in mine)


def send_home(rows):
    experts = lax.axis_size("expert")
    shaped = rows.reshape(experts, rows.shape[0] // experts, rows.shape[1])
    return lax.all_to_all(shaped, "expert", split_axis=0, concat_axis=0, tiled=True)


def local(tokens, routes, mix_weights, cotangent, w_gate, w_up, w_down):
    experts = lax.axis_size("expert")
    w_gate, w_up, w_down = w_gate[0], w_up[0], w_down[0]

    home_weight = jnp.sum(
        jnp.where(
            routes[None, :, :] == jnp.arange(experts, dtype=routes.dtype)[:, None, None],
            mix_weights[None, :, :],
            0.0,
        ),
        axis=2,
    )
    features = tokens.shape[1]
    dy_home = (home_weight[:, :, None] * cotangent.astype(jnp.float32)[None]).astype(jnp.bfloat16)
    sent = jnp.concatenate([jnp.broadcast_to(tokens[None], dy_home.shape), dy_home], axis=2)
    got = lax.all_to_all(sent, "expert", split_axis=0, concat_axis=0, tiled=True)
    got = got.reshape(-1, 2 * features)
    x_part, dy_part = got[:, :features], got[:, features:]
    row_weight = lax.all_to_all(
        home_weight[:, None, :], "expert", split_axis=0, concat_axis=0, tiled=True
    ).reshape(-1, 1)

    def partial(rows, weights):
        return jnp.dot(rows, weights, preferred_element_type=jnp.float32).astype(jnp.bfloat16)

    parts = (partial(x_part, w_gate), partial(x_part, w_up), partial(dy_part, w_down))
    x_home = lax.all_gather(tokens, "shard", axis=1, tiled=True)
    cot_home = lax.all_gather(cotangent, "shard", axis=1, tiled=True)
    x_home, cot_home, parts = lax.optimization_barrier((x_home, cot_home, parts))
    (hidden, d_gate, d_up), (hidden_all, d_gate_all, d_up_all) = to_hidden(parts)
    col_contract = (((1,), (1,)), ((), ()))
    out_rows = lax.dot_general(
        hidden_all, w_down, col_contract, preferred_element_type=jnp.float32
    ).astype(jnp.bfloat16)
    dx_rows = lax.dot_general(d_gate_all, w_gate, col_contract, preferred_element_type=jnp.float32)
    dx_rows = dx_rows + lax.dot_general(
        d_up_all, w_up, col_contract, preferred_element_type=jnp.float32
    )
    dx_rows = dx_rows.astype(jnp.bfloat16)
    out_home = send_home(out_rows)
    dx_home = send_home(dx_rows)
    layer_out = jnp.sum(home_weight[:, :, None] * out_home.astype(jnp.float32), axis=0).astype(
        jnp.bfloat16
    )
    grad_tokens = jnp.sum(dx_home.astype(jnp.float32), axis=0).astype(jnp.bfloat16)

    x_rows = lax.all_gather(x_home, "expert", axis=0, tiled=True)
    x_rows = jnp.where(row_weight > 0, x_rows, jnp.zeros_like(x_rows))
    cot_rows = lax.all_gather(cot_home, "expert", axis=0, tiled=True)
    dy_rows = (row_weight * cot_rows.astype(jnp.float32)).astype(jnp.bfloat16)
    row_contract = (((0,), (0,)), ((), ()))

    def gradient(rows, slices):
        return lax.dot_general(
            rows, slices, row_contract, preferred_element_type=jnp.float32
        ).astype(jnp.bfloat16)

    grad_down = gradient(dy_rows, hidden)
    grad_gate = gradient(x_rows, d_gate)
    grad_up = gradient(x_rows, d_up)
    return (layer_out, grad_tokens, grad_gate[None], grad_up[None], grad_down[None])


def solution(mesh):
    return jax.shard_map(
        local,
        mesh=mesh,
        in_specs=(
            P("expert", "shard"),
            P("expert", None),
            P("expert", None),
            P("expert", "shard"),
            P("expert", "shard", None),
            P("expert", "shard", None),
            P("expert", "shard", None),
        ),
        out_specs=(
            P("expert", "shard"),
            P("expert", "shard"),
            P("expert", None, "shard"),
            P("expert", None, "shard"),
            P("expert", None, "shard"),
        ),
        check_vma=False,
    )
```

```python
import functools

import jax
import jax.numpy as jnp
from jax import lax
from jax.experimental import pallas as pl
from jax.experimental.pallas import tpu as pltpu
from jax.sharding import PartitionSpec as P

MESH = pl.DeviceIdType.MESH
VMEM_BUDGET = 56 * 1024 * 1024
BLOCKS = 16
LAG = 1


def place(shards):
    me = lax.axis_index("shard")
    chip = me // 2
    core = me % 2
    return me, chip, core, me + 1 - 2 * core


def greet(me, chip, sibling, line):
    barrier = pltpu.get_barrier_semaphore()
    pl.semaphore_signal(barrier, inc=1, device_id={"shard": sibling}, device_id_type=MESH)

    @pl.when(chip > 0)
    def _():
        pl.semaphore_signal(barrier, inc=1, device_id={"shard": me - 2}, device_id_type=MESH)

    @pl.when(chip < line - 1)
    def _():
        pl.semaphore_signal(barrier, inc=1, device_id={"shard": me + 2}, device_id_type=MESH)

    peers = jnp.where(chip > 0, 2, 1) + jnp.where(chip < line - 1, 1, 0)
    pl.semaphore_wait(barrier, peers)


def exchange_kernel(
    shards, blocks, p0, p1, p2, mine, full, stage, core_in, line_in,
    load_sem, core_send, core_recv, line_send, line_recv,
    ring_right, ring_left, ring_recv, pair_send, pair_recv, own_sem,
):
    line = shards // 2
    rows, width = stage.shape[3], stage.shape[4]
    me, chip, core, sibling = place(shards)
    left_half = 2 * chip < line
    greet(me, chip, sibling, line)

    def rows_of(r):
        return pl.ds(pl.multiple_of(r * rows, rows), rows)

    def cols_of(shard):
        return pl.ds(pl.multiple_of(shard * width, 128), width)

    def turn(j):
        return jnp.where(left_half, line - 1 - j, j)

    def load(part, r, d, m):
        return pltpu.make_async_copy(
            part.at[rows_of(r), cols_of(2 * d + core)], stage.at[r, d, m], load_sem.at[r, d, m]
        )

    def swap(part, r, d, m):
        return pltpu.make_async_remote_copy(
            src_ref=part.at[rows_of(r), cols_of(2 * d + 1 - core)],
            dst_ref=core_in.at[r, d, m],
            send_sem=core_send.at[r, d, m],
            recv_sem=core_recv.at[r, d, m],
            device_id={"shard": sibling},
            device_id_type=MESH,
        )

    def pass_on(r, d, slot, to):
        return pltpu.make_async_remote_copy(
            src_ref=stage.at[r, d],
            dst_ref=line_in.at[r, slot],
            send_sem=line_send.at[r, d],
            recv_sem=line_recv.at[r, slot],
            device_id={"shard": to},
            device_id_type=MESH,
        )

    def block(r, shard):
        return full.at[:, rows_of(r), cols_of(shard)]

    def send(src, r, origin, way):
        return pltpu.make_async_remote_copy(
            src_ref=src,
            dst_ref=block(r, 2 * origin + core),
            send_sem=(ring_right if way > 0 else ring_left).at[r, origin],
            recv_sem=ring_recv.at[r, origin],
            device_id={"shard": me + 2 * way},
            device_id_type=MESH,
        )

    def share(src, r, origin):
        return pltpu.make_async_remote_copy(
            src_ref=src,
            dst_ref=block(r, 2 * origin + core),
            send_sem=pair_send.at[r, origin],
            recv_sem=pair_recv.at[r, origin],
            device_id={"shard": sibling},
            device_id_type=MESH,
        )

    def keep(r):
        return pltpu.make_async_copy(mine.at[:, rows_of(r)], block(r, me), own_sem.at[r])

    def wide(value):
        return value.astype(jnp.float32)

    def begin(r):
        for j in range(line):
            for m, part in enumerate((p0, p1, p2)):
                swap(part, r, turn(j), m).start()
                load(part, r, turn(j), m).start()

    def arrived(r, d):
        for m in range(3):
            load(p0, r, d, m).wait()
            swap(p0, r, d, m).wait_recv()

    def relay(r):
        for j in range(line):
            d = turn(j)

            @pl.when(chip != d)
            def _(d=d):
                rightward = chip < d
                slot = jnp.where(rightward, d + 1, d)
                to = jnp.where(rightward, me + 2, me - 2)
                at_end = jnp.where(rightward, chip, line - 1 - chip) == 0
                arrived(r, d)

                @pl.when(at_end)
                def _():
                    for m in range(3):
                        stage[r, d, m] = (wide(stage[r, d, m]) + wide(core_in[r, d, m])).astype(
                            stage.dtype
                        )

                @pl.when(jnp.logical_not(at_end))
                def _():
                    pass_on(r, d, slot, to).wait_recv()
                    for m in range(3):
                        stage[r, d, m] = (
                            wide(stage[r, d, m]) + wide(core_in[r, d, m]) + wide(line_in[r, slot, m])
                        ).astype(stage.dtype)

                pass_on(r, d, slot, to).start()

    def finish(r):
        arrived(r, chip)

        def total(m):
            return wide(stage[r, chip, m]) + wide(core_in[r, chip, m])

        def store(gate_pre, up_pre, d_hidden):
            sigmoid_gate = jax.nn.sigmoid(gate_pre)
            active = gate_pre * sigmoid_gate
            slope = sigmoid_gate * (1.0 + gate_pre * (1.0 - sigmoid_gate))
            mine[0, rows_of(r)] = (active * up_pre).astype(mine.dtype)
            mine[1, rows_of(r)] = (d_hidden * up_pre * slope).astype(mine.dtype)
            mine[2, rows_of(r)] = (d_hidden * active).astype(mine.dtype)

        @pl.when(chip == 0)
        def _():
            pass_on(r, chip, chip, sibling).wait_recv()
            store(*[total(m) + wide(line_in[r, chip, m]) for m in range(3)])

        @pl.when(chip == line - 1)
        def _():
            pass_on(r, chip, chip + 1, sibling).wait_recv()
            store(*[total(m) + wide(line_in[r, chip + 1, m]) for m in range(3)])

        @pl.when(jnp.logical_and(chip > 0, chip < line - 1))
        def _():
            pass_on(r, chip, chip, sibling).wait_recv()
            pass_on(r, chip, chip + 1, sibling).wait_recv()
            store(
                *[
                    total(m) + wide(line_in[r, chip, m]) + wide(line_in[r, chip + 1, m])
                    for m in range(3)
                ]
            )

        src = mine.at[:, rows_of(r)]

        @pl.when(chip < line - 1)
        def _():
            send(src, r, chip, 1).start()

        @pl.when(chip > 0)
        def _():
            send(src, r, chip, -1).start()

        share(src, r, chip).start()
        keep(r).start()

    def forward(r, step):
        @pl.when(chip - step >= 0)
        def _():
            origin = chip - step
            got = block(r, 2 * origin + core)
            send(got, r, origin, 1).wait_recv()

            @pl.when(chip < line - 1)
            def _():
                send(got, r, origin, 1).start()

            share(got, r, origin).start()

        @pl.when(chip + step < line)
        def _():
            origin = chip + step
            got = block(r, 2 * origin + core)
            send(got, r, origin, -1).wait_recv()

            @pl.when(chip > 0)
            def _():
                send(got, r, origin, -1).start()

            share(got, r, origin).start()

    begin(0)

    def advance(i, carry):
        @pl.when(i + 1 < blocks)
        def _():
            begin(i + 1)

        @pl.when(i < blocks)
        def _():
            relay(i)

        @pl.when(jnp.logical_and(i >= LAG, i - LAG < blocks))
        def _():
            finish(i - LAG)

        for step in range(1, line):
            @pl.when(jnp.logical_and(i >= LAG + step, i - LAG - step < blocks))
            def _(step=step):
                forward(i - LAG - step, step)
        return carry

    lax.fori_loop(0, blocks + LAG + line - 1, advance, 0)

    def settle(r, carry):
        keep(r).wait()
        for d in range(line):
            got = block(r, 2 * d + core)
            share(got, r, d).wait()
            for m in range(3):
                swap(p0, r, d, m).wait_send()

            @pl.when(chip != d)
            def _(d=d):
                pass_on(r, d, d, sibling).wait_send()

            @pl.when(jnp.logical_and(d <= chip, chip < line - 1))
            def _(d=d, got=got):
                send(got, r, d, 1).wait_send()

            @pl.when(jnp.logical_and(d >= chip, chip > 0))
            def _(d=d, got=got):
                send(got, r, d, -1).wait_send()
        return carry

    lax.fori_loop(0, blocks, settle, 0)


def exchange(shards, parts):
    rows_all, cols = parts[0].shape
    rows, width, line = rows_all // BLOCKS, cols // shards, shards // 2
    dma = pltpu.SemaphoreType.DMA
    pairs, triples = (BLOCKS, line), (BLOCKS, line, 3)
    chunks = (BLOCKS, line, 3, rows, width)
    return pl.pallas_call(
        functools.partial(exchange_kernel, shards, BLOCKS),
        out_shape=(
            jax.ShapeDtypeStruct((3, rows_all, width), jnp.bfloat16),
            jax.ShapeDtypeStruct((3, rows_all, cols), jnp.bfloat16),
        ),
        in_specs=[pl.BlockSpec(memory_space=pl.ANY)] * 3,
        out_specs=(pl.BlockSpec(memory_space=pltpu.VMEM), pl.BlockSpec(memory_space=pl.ANY)),
        scratch_shapes=[
            pltpu.VMEM(chunks, jnp.bfloat16),
            pltpu.VMEM(chunks, jnp.bfloat16),
            pltpu.VMEM((BLOCKS, line + 1, 3, rows, width), jnp.bfloat16),
            dma(triples),
            dma(triples),
            dma(triples),
            dma(pairs),
            dma((BLOCKS, line + 1)),
            dma(pairs),
            dma(pairs),
            dma(pairs),
            dma(pairs),
            dma(pairs),
            dma((BLOCKS,)),
        ],
        compiler_params=pltpu.CompilerParams(
            collective_id=0, has_side_effects=True, vmem_limit_bytes=VMEM_BUDGET
        ),
        cost_estimate=pl.CostEstimate(
            flops=200_000_000_000, bytes_accessed=800_000_000, transcendentals=0
        ),
    )(*parts)


def use_kernels(shards, rows, cols):
    line = shards // 2
    chunk = 3 * rows * (cols // shards)
    need = chunk * (2 * (3 * line + 1) + 4)
    return shards % 2 == 0 and shards > 2 and need < VMEM_BUDGET - 8 * 1024 * 1024


def activate(gate_pre, up_pre, d_hidden):
    sigmoid_gate = jax.nn.sigmoid(gate_pre)
    active = gate_pre * sigmoid_gate
    hidden = active * up_pre
    d_gate = d_hidden * up_pre * sigmoid_gate * (1.0 + gate_pre * (1.0 - sigmoid_gate))
    return tuple(value.astype(jnp.bfloat16) for value in (hidden, d_gate, d_hidden * active))


def to_hidden(parts):
    shards = lax.axis_size("shard")
    if use_kernels(shards, *parts[0].shape):
        return exchange(shards, parts)
    sums = [
        lax.psum_scatter(part, "shard", scatter_dimension=1, tiled=True).astype(jnp.float32)
        for part in parts
    ]
    mine = activate(*sums)
    return mine, tuple(lax.all_gather(part, "shard", axis=1, tiled=True) for part in mine)


def send_home(rows):
    experts = lax.axis_size("expert")
    shaped = rows.reshape(experts, rows.shape[0] // experts, rows.shape[1])
    return lax.all_to_all(shaped, "expert", split_axis=0, concat_axis=0, tiled=True)


def local(tokens, routes, mix_weights, cotangent, w_gate, w_up, w_down):
    experts = lax.axis_size("expert")
    w_gate, w_up, w_down = w_gate[0], w_up[0], w_down[0]

    home_weight = jnp.sum(
        jnp.where(
            routes[None, :, :] == jnp.arange(experts, dtype=routes.dtype)[:, None, None],
            mix_weights[None, :, :],
            0.0,
        ),
        axis=2,
    )
    features = tokens.shape[1]
    dy_home = (home_weight[:, :, None] * cotangent.astype(jnp.float32)[None]).astype(jnp.bfloat16)
    sent = jnp.concatenate([jnp.broadcast_to(tokens[None], dy_home.shape), dy_home], axis=2)
    got = lax.all_to_all(sent, "expert", split_axis=0, concat_axis=0, tiled=True)
    got = got.reshape(-1, 2 * features)
    x_part, dy_part = got[:, :features], got[:, features:]
    row_weight = lax.all_to_all(
        home_weight[:, None, :], "expert", split_axis=0, concat_axis=0, tiled=True
    ).reshape(-1, 1)

    def partial(rows, weights):
        return jnp.dot(rows, weights, preferred_element_type=jnp.float32).astype(jnp.bfloat16)

    parts = (partial(x_part, w_gate), partial(x_part, w_up), partial(dy_part, w_down))
    x_home = lax.all_gather(tokens, "shard", axis=1, tiled=True)
    cot_home = lax.all_gather(cotangent, "shard", axis=1, tiled=True)
    x_home, cot_home, parts = lax.optimization_barrier((x_home, cot_home, parts))
    (hidden, d_gate, d_up), (hidden_all, d_gate_all, d_up_all) = to_hidden(parts)
    col_contract = (((1,), (1,)), ((), ()))
    out_rows = lax.dot_general(
        hidden_all, w_down, col_contract, preferred_element_type=jnp.float32
    ).astype(jnp.bfloat16)
    dx_rows = lax.dot_general(d_gate_all, w_gate, col_contract, preferred_element_type=jnp.float32)
    dx_rows = dx_rows + lax.dot_general(
        d_up_all, w_up, col_contract, preferred_element_type=jnp.float32
    )
    dx_rows = dx_rows.astype(jnp.bfloat16)
    out_home = send_home(out_rows)
    dx_home = send_home(dx_rows)
    layer_out = jnp.sum(home_weight[:, :, None] * out_home.astype(jnp.float32), axis=0).astype(
        jnp.bfloat16
    )
    grad_tokens = jnp.sum(dx_home.astype(jnp.float32), axis=0).astype(jnp.bfloat16)

    x_rows = lax.all_gather(x_home, "expert", axis=0, tiled=True)
    x_rows = jnp.where(row_weight > 0, x_rows, jnp.zeros_like(x_rows))
    cot_rows = lax.all_gather(cot_home, "expert", axis=0, tiled=True)
    dy_rows = (row_weight * cot_rows.astype(jnp.float32)).astype(jnp.bfloat16)
    row_contract = (((0,), (0,)), ((), ()))

    def gradient(rows, slices):
        return lax.dot_general(
            rows, slices, row_contract, preferred_element_type=jnp.float32
        ).astype(jnp.bfloat16)

    grad_down = gradient(dy_rows, hidden)
    grad_gate = gradient(x_rows, d_gate)
    grad_up = gradient(x_rows, d_up)
    return (layer_out, grad_tokens, grad_gate[None], grad_up[None], grad_down[None])


def solution(mesh):
    return jax.shard_map(
        local,
        mesh=mesh,
        in_specs=(
            P("expert", "shard"),
            P("expert", None),
            P("expert", None),
            P("expert", "shard"),
            P("expert", "shard", None),
            P("expert", "shard", None),
            P("expert", "shard", None),
        ),
        out_specs=(
            P("expert", "shard"),
            P("expert", "shard"),
            P("expert", None, "shard"),
            P("expert", None, "shard"),
            P("expert", None, "shard"),
        ),
        check_vma=False,
    )
```
